32 devices in a mesh: req: 4 (over y, x), vocab: 8 (over z, core).
Axes of the slice: x: 2, y: 2, z: 4, core: 2. Of those that a mesh axis runs over, the one named last changes fastest.
Arguments:
- hidden: bfloat16 [8192, 4096], P('req', 'vocab'), may hold values from -320 to 320
- gain: float32 [4096], replicated, may hold values from 0.5 to 1.5
- head: bfloat16 [4096, 32768], P(None, ('req', 'vocab'))
- targets: int32 [8192], P('req'), may hold values from 0 to 32767
- lengths: int32 [4, 4], P('req'), may hold values from 1 to 1280, 2048 in all within a row
Outputs:
- token_logprob: float32 [8192], P(('req', 'vocab'))
- token_entropy: float32 [8192], P(('req', 'vocab'))
- seq_logprob: float32 [12], P('req')
- seq_entropy: float32 [12], P('req')
The draws below stay inside these ranges and needn't reach their ends.
Inputs may be any that keep to these rules, and one draw needn't show every extreme that they name: lengths[q, 3] counts the empty slots at the end of index q's rows.
All inputs are finite; a program needn't handle non-finite values.
Results may differ from the reference program's by a relative error of at most 0.0012.
Values may be sent and summed in bfloat16 or wider, within the bound.
No kernel may reach another device: no remote copies, remote signals or barrier semaphores. Data moves between devices by JAX's collectives and lax.ppermute only.
A program may use at most 128 MiB of HBM per device.

```python
import math
import jax
import jax.numpy as jnp
import numpy as np
from jax import lax

D = 4096
VOCAB = 32768
SEQ_DEV = 3
ROWS_DEV = 2048
ROWS = 8192
SEQS = 12
MOST = 1280
N_REQ = 4


def base_hidden(key):
    noise = jax.random.normal(jax.random.fold_in(key, 1), (ROWS, D), jnp.float32)
    row_scale = jnp.exp(jax.random.uniform(jax.random.fold_in(key, 2), (ROWS,), jnp.float32, 0.0, math.log(10.0)))
    col_rough = jax.random.uniform(jax.random.fold_in(key, 3), (D,), jnp.float32, 0.6, 1.4)
    col_scale = jnp.exp(jnp.arange(D, dtype=jnp.float32) * (math.log(3.0) / D)) * col_rough
    return noise * row_scale[:, None] * col_scale[None, :]


def draw_hidden(key, part):
    return base_hidden(jax.random.fold_in(key, 11)).astype(jnp.bfloat16)


def draw_head(key, part):
    weights = jax.random.normal(jax.random.fold_in(key, 23), (D, VOCAB), jnp.float32) * (3.0 / math.sqrt(D))
    return weights.astype(jnp.bfloat16)


def touch_ends(values, stream_key, smallest, top_value):
    dims = values.shape
    spot = [jax.random.randint(jax.random.fold_in(stream_key, axis), (), 0, dims[axis]) for axis in range(len(dims))]
    values = values.at[tuple(spot)].set(smallest)
    longest = dims.index(max(dims))
    spot[longest] = (spot[longest] + 1) % dims[longest]
    return values.at[tuple(spot)].set(top_value)


def rank_bounds(number_of, lean):
    loads = [(1 << 20) // math.isqrt(grade ** lean) + 1 for grade in range(1, number_of + 1)]
    scale = 1 + sum(loads) // (1 << 30)
    return np.cumsum(np.array([max(1, weight // scale) for weight in loads]))


def ranked_ids(own_key, dims, amount, skew):
    table = rank_bounds(amount, skew)
    ticket = jax.random.randint(jax.random.fold_in(own_key, 1), dims, 0, int(table[amount - 1]))
    rank = jnp.searchsorted(jnp.asarray(table, jnp.int32), ticket, side="right")
    return jax.random.permutation(jax.random.fold_in(own_key, 2), amount)[rank].astype(jnp.int32)


def split_up(number_of, total, limit, lean):
    loads = [(1 << 20) // math.isqrt(grade ** lean) + 1 for grade in range(2, number_of + 1)]
    surplus, given = total - limit - (number_of - 1), [1] * (number_of - 1)
    while surplus > 0:
        free = [i for i in range(number_of - 1) if given[i] < limit]
        mass, remaining = sum([loads[i] for i in free]), surplus
        for i in free:
            extra = min(limit - given[i], max(1, remaining * loads[i] // mass), surplus)
            given[i] = given[i] + extra
            surplus = surplus - extra
    return np.array([limit] + given)


def uneven(stream_key, amount, total, bound, slope):
    if amount == 2:
        one = jax.random.randint(stream_key, (), max(1, total - bound), min(bound, total - 1) + 1)
        return jnp.stack([one, total - one])
    sizes = jnp.asarray(split_up(amount, total, bound, slope), jnp.int32)
    couples = (amount - 1) // 2
    donor, receiver = sizes[1:1 + 2 * couples:2], sizes[2:2 + 2 * couples:2]
    slack = jnp.minimum(donor - 1, bound - receiver)
    shifted = jax.random.randint(jax.random.fold_in(stream_key, 1), (couples,), 0, 1 << 20) % (slack + 1)
    sizes = sizes.at[1:1 + 2 * couples:2].set(donor - shifted).at[2:2 + 2 * couples:2].set(receiver + shifted)
    return sizes[jax.random.permutation(jax.random.fold_in(stream_key, 2), amount)]


def setup_inputs(seed: int = 0) -> dict:
    arg_keys = jax.random.split(jax.random.key(seed), 6)
    hidden = draw_hidden(jax.random.fold_in(arg_keys[5], 71), 0)
    gain = jnp.clip(1.0 + 0.1 * jax.random.normal(arg_keys[1], (D,), jnp.float32), 0.5, 1.5)
    head = draw_head(jax.random.fold_in(arg_keys[5], 71), 0)
    targets = touch_ends(ranked_ids(arg_keys[3], (ROWS,), VOCAB, 2), jax.random.fold_in(arg_keys[3], 3), 0, VOCAB - 1).astype(jnp.int32)
    lengths = jax.vmap(lambda own: uneven(own, SEQ_DEV + 1, ROWS_DEV, MOST, 2))(jax.random.split(arg_keys[4], N_REQ)).reshape((N_REQ, SEQ_DEV + 1)).astype(jnp.int32)
    return {"hidden": hidden, "gain": gain, "head": head, "targets": targets, "lengths": lengths}


EPS = 1e-05

def reference(hidden, gain, head, targets, lengths):
    values = hidden.astype(jnp.float32)
    mean_sq = lax.optimization_barrier(jnp.sum(values * values, axis=1)) / D
    normed = (values * lax.rsqrt(mean_sq + EPS)[:, None] * gain[None, :]).astype(jnp.bfloat16)
    block = min(512, ROWS_DEV)
    count = ROWS // block

    def one_block(block_index):
        start = block_index * block
        rows_blk = lax.dynamic_slice_in_dim(normed, start, block, 0)
        logits = jnp.dot(rows_blk, head, preferred_element_type=jnp.float32)
        wanted = lax.dynamic_slice_in_dim(targets, start, block, 0)
        peak = lax.optimization_barrier(jnp.max(logits, axis=1))
        weights = jnp.exp(logits - peak[:, None])
        total = lax.optimization_barrier(jnp.sum(weights, axis=1))
        moment = lax.optimization_barrier(jnp.sum(weights * logits, axis=1))
        picked = jnp.take_along_axis(logits, wanted[:, None], axis=1)[:, 0]
        log_total = peak + jnp.log(total)
        return (picked - log_total, log_total - moment / total)
    logprob, entropy = lax.map(one_block, jnp.arange(count, dtype=jnp.int32))
    logprob = logprob.reshape(N_REQ, ROWS_DEV)
    entropy = entropy.reshape(N_REQ, ROWS_DEV)
    seq_lens = lengths[:, :SEQ_DEV].astype(jnp.int32)
    ends = jnp.cumsum(seq_lens, axis=1).astype(jnp.int32)
    starts = ends - seq_lens
    local = jnp.arange(ROWS_DEV, dtype=jnp.int32)
    valid = local[None, :] < ends[:, -1:]
    logprob = jnp.where(valid, logprob, 0.0)
    entropy = jnp.where(valid, entropy, 0.0)
    member = ((local[None, None, :] >= starts[:, :, None]) & (local[None, None, :] < ends[:, :, None])).astype(jnp.float32)
    divisor = seq_lens.astype(jnp.float32)
    seq_lp = lax.optimization_barrier(jnp.sum(member * logprob[:, None, :], axis=2)) / divisor
    seq_ent = lax.optimization_barrier(jnp.sum(member * entropy[:, None, :], axis=2)) / divisor
    return (logprob.reshape(ROWS), entropy.reshape(ROWS), seq_lp.reshape(SEQS), seq_ent.reshape(SEQS))
```

```python
import functools
import jax
import jax.numpy as jnp
from jax import lax
from jax.experimental import pallas as pl
from jax.experimental.pallas import tpu as pltpu
from jax.sharding import PartitionSpec as P


def round_up(n, m):
    return (n + m - 1) // m * m


def stats_kernel(tiles, groups, n_pieces, n_heads, *refs):
    kofs, colbase, rs_ref, tgt_ref = refs[:4]
    pieces = refs[4 : 4 + n_pieces]
    heads = refs[4 + n_pieces : 4 + n_pieces + n_heads]
    out_ref, x_scr, h_scr, m_scr, s_scr, w_scr, p_scr, x_sem, h_sem = refs[4 + n_pieces + n_heads :]
    r, i = pl.program_id(0), pl.program_id(1)
    n_tiles, n_steps = len(tiles), sum(g[2] for g in groups)
    width = h_scr.shape[3]
    step = r * n_steps + i
    xs = lax.rem(r, x_scr.shape[0])
    hs = lax.rem(step, 2) if n_steps > 1 else 0

    def row_copies(k, slot):
        return [
            pltpu.make_async_copy(
                pieces[a].at[pl.ds(src, rows)],
                x_scr.at[slot, pl.ds(dst, rows), pl.ds(pl.multiple_of(kofs[j], 128), pieces[a].shape[1])],
                x_sem.at[slot],
            )
            for a, j, src, rows, dst in tiles[k]
        ]

    def head_copies(g, block, slot):
        return [
            pltpu.make_async_copy(
                heads[groups[g][which]].at[:, pl.ds(pl.multiple_of(block * width, width), width)],
                h_scr.at[slot, which],
                h_sem.at[slot],
            )
            for which in range(2)
        ]

    def start_head(at, slot):
        first = 0
        for g, (_, _, blocks) in enumerate(groups):
            @pl.when((at >= first) & (at < first + blocks))
            def _(g=g, first=first):
                for copy in head_copies(g, at - first, slot):
                    copy.start()
            first += blocks

    def start_rows(at, slot):
        for k in range(n_tiles):
            @pl.when(at == k)
            def _(k=k):
                for copy in row_copies(k, slot):
                    copy.start()

    @pl.when(step == 0)
    def _():
        start_rows(0, 0)
        start_head(0, 0)

    @pl.when(i == 0)
    def _():
        if n_tiles > 1:
            @pl.when(r + 1 < n_tiles)
            def _():
                start_rows(r + 1, lax.rem(r + 1, 2))
        m_scr[...] = jnp.full(m_scr.shape, -jnp.inf, jnp.float32)
        s_scr[...] = jnp.zeros(s_scr.shape, jnp.float32)
        w_scr[...] = jnp.zeros(w_scr.shape, jnp.float32)
        p_scr[...] = jnp.zeros(p_scr.shape, jnp.float32)
        for k in range(n_tiles):
            @pl.when(r == k)
            def _(k=k):
                for copy in row_copies(k, xs):
                    copy.wait()

    if n_steps > 1:
        @pl.when(step + 1 < n_tiles * n_steps)
        def _():
            start_head(lax.rem(i + 1, n_steps), lax.rem(step + 1, 2))
    @pl.when((i == 0) & (r == 0) if n_steps == 1 else i >= 0)
    def _():
        for copy in head_copies(0, 0, hs):
            copy.wait()

    rows = x_scr.shape[1]
    sub = 64
    lane = lax.broadcasted_iota(jnp.int32, (sub, 128), 1)
    for which in range(2):
        raw = jnp.dot(x_scr[xs], h_scr[hs, which], preferred_element_type=jnp.float32)
        base = colbase[i * 2 + which]
        for at in range(0, rows, sub):
            here = pl.ds(at, sub)
            scale = rs_ref[here, :]
            wanted = tgt_ref[here, :] - base - lane
            parts = [raw[at : at + sub, c : c + 128] * scale for c in range(0, width, 128)]
            old = m_scr[here, :]
            new = functools.reduce(jnp.maximum, parts, old)
            fade = jnp.exp(old - new)
            total, moment, picked = s_scr[here, :] * fade, w_scr[here, :] * fade, p_scr[here, :]
            for c, part in enumerate(parts):
                weight = jnp.exp(part - new)
                total += weight
                moment += weight * part
                picked = jnp.where(wanted == c * 128, part, picked)
            m_scr[here, :], s_scr[here, :], w_scr[here, :], p_scr[here, :] = new, total, moment, picked

    @pl.when(i == n_steps - 1)
    def _():
        peak_t = m_scr[...].T
        peak = jnp.max(peak_t, axis=0, keepdims=True)
        fade = jnp.exp(peak_t - peak)
        out_ref[0:1, :] = peak
        out_ref[1:2, :] = jnp.sum(s_scr[...].T * fade, axis=0, keepdims=True)
        out_ref[2:3, :] = jnp.sum(w_scr[...].T * fade, axis=0, keepdims=True)
        out_ref[3:4, :] = jnp.sum(p_scr[...].T, axis=0, keepdims=True)


def stats(tiles, tile_rows, groups, kofs, colbase, scale, wanted, pieces, heads):
    rows = round_up(tile_rows, 128)
    n_tiles, n_steps = len(tiles), sum(g[2] for g in groups)
    depth = heads[0].shape[0]
    width = min([256] + [h.shape[1] for h in heads])

    def column(v):
        return jnp.pad(v.reshape(n_tiles, tile_rows), ((0, 0), (0, rows - tile_rows))).reshape(-1, 1)

    row_block = pl.BlockSpec((rows, 1), lambda r, i: (r, 0))
    out = pl.pallas_call(
        functools.partial(stats_kernel, tiles, groups, len(pieces), len(heads)),
        grid=(n_tiles, n_steps),
        in_specs=[pl.BlockSpec(memory_space=pltpu.SMEM)] * 2
        + [row_block] * 2
        + [pl.BlockSpec(memory_space=pl.ANY)] * (len(pieces) + len(heads)),
        out_specs=pl.BlockSpec((4, rows), lambda r, i: (0, r)),
        out_shape=jax.ShapeDtypeStruct((4, n_tiles * rows), jnp.float32),
        scratch_shapes=[
            pltpu.VMEM((min(n_tiles, 2), rows, depth), jnp.bfloat16),
            pltpu.VMEM((min(n_steps, 2), 2, depth, width), jnp.bfloat16),
        ]
        + [pltpu.VMEM((rows, 128), jnp.float32)] * 4
        + [pltpu.SemaphoreType.DMA((min(n_tiles, 2),)), pltpu.SemaphoreType.DMA((min(n_steps, 2),))],
        compiler_params=pltpu.CompilerParams(
            dimension_semantics=("arbitrary", "arbitrary"), vmem_limit_bytes=48 * 1024 * 1024
        ),
        cost_estimate=pl.CostEstimate(
            flops=2 * n_tiles * rows * n_steps * 2 * width * depth,
            bytes_accessed=2 * depth * (n_tiles * rows + 2 * width * n_steps),
            transcendentals=n_tiles * rows * n_steps * 2 * width,
        ),
    )(kofs, colbase, column(scale), column(wanted), *pieces, *heads)
    return out.reshape(4, n_tiles, rows)[:, :, :tile_rows].reshape(4, n_tiles * tile_rows)


EPS = 1e-05
SHRINK = 2.0**-9


def merge(stats):
    peak, total, moment, picked = (stats[:, k] for k in range(4))
    best = jnp.max(peak, axis=0)
    fade = jnp.exp(peak - best[None])
    return jnp.stack(
        [best, jnp.sum(total * fade, axis=0), jnp.sum(moment * fade, axis=0), jnp.sum(picked, axis=0)]
    )


def shards(hidden, gain, head, targets, lengths):
    n_req, n_vocab = lax.axis_size("req"), lax.axis_size("vocab")
    q, v = lax.axis_index("req"), lax.axis_index("vocab")
    spots = n_vocab // 2
    s, c = v // 2, v % 2
    rows, feats = hidden.shape
    depth, cols = head.shape
    blk, half = rows // n_vocab, rows // 2
    cut = half - blk
    every = ("req", "vocab")

    def move(x, where):
        pairs = [
            (a * n_vocab + b, where(a, b)) for a in range(n_req) for b in range(n_vocab)
        ]
        return lax.ppermute(x, every, pairs)

    def to_core(x):
        return move(x, lambda a, b: a * n_vocab + (b ^ 1))

    def to_x(x):
        return move(x, lambda a, b: (a ^ 1) * n_vocab + b)

    def to_y(x):
        return move(x, lambda a, b: (a ^ 2) * n_vocab + b)

    def to_z(x):
        return move(x, lambda a, b: a * n_vocab + (b + 2) % n_vocab)

    def ring(x):
        out = [x]
        for _ in range(spots - 1):
            out.append(to_z(out[-1]))
        return out

    n_far = max(1, min(4, cols // 128))
    far_cols = cols // n_far
    far = [to_x(head[:, k * far_cols : (k + 1) * far_cols]) for k in range(n_far)]

    values = hidden.astype(jnp.float32)
    own_gain = lax.dynamic_slice_in_dim(gain, v * feats, feats) * SHRINK
    scaled = (values * own_gain[None, :]).astype(jnp.bfloat16).reshape(spots, 2, blk, feats)
    mine = lax.dynamic_index_in_dim(scaled, c, 1, keepdims=False).reshape(half, feats)
    other = lax.dynamic_index_in_dim(scaled, 1 - c, 1, keepdims=False).reshape(half, feats)
    got = to_core(other)
    piece = jnp.where(
        c == 0, jnp.concatenate([mine, got], axis=1), jnp.concatenate([got, mine], axis=1)
    )
    a0, b0 = piece[:cut], piece[cut:]
    yb0 = to_y(b0)
    a_pieces = ring(a0)
    ya_pieces = [to_y(p) for p in a_pieces]
    b_pieces = ring(b0)
    yb_pieces = ring(yb0)

    near = to_core(head)
    far_near = [to_core(h) for h in far]

    square = lax.psum(jnp.sum(values * values, axis=1), "vocab")
    scale = lax.rsqrt(square / depth + EPS) * (1.0 / SHRINK)
    scale = lax.dynamic_index_in_dim(scale.reshape(spots, 2, blk), c, 1, keepdims=False).reshape(half)
    wanted = lax.dynamic_index_in_dim(targets.reshape(spots, 2, blk), c, 1, keepdims=False).reshape(half)
    y_side = to_y(jnp.stack([scale, wanted.astype(jnp.float32)]))
    y_scale, y_wanted = y_side[0], y_side[1].astype(jnp.int32)

    kofs = (s + spots - jnp.arange(spots, dtype=jnp.int32)) % spots * (2 * feats)
    own_base = (q * n_vocab + v) * cols
    pair_base = (q * n_vocab + (v ^ 1)) * cols
    far_base = ((q ^ 1) * n_vocab + v) * cols
    far_pair_base = ((q ^ 1) * n_vocab + (v ^ 1)) * cols
    groups = [(head, near, own_base, pair_base)] + [
        (far[k], far_near[k], far_base + k * far_cols, far_pair_base + k * far_cols)
        for k in range(n_far)
    ]

    def call(row_sets, chosen):
        tiles, arrays, scales, wants = [], [], [], []
        for sets in row_sets:
            at, tile = 0, []
            for pieces, set_scale, set_wanted in sets:
                n = set_scale.shape[0]
                for j, p in enumerate(pieces):
                    tile.append((len(arrays), j, 0, n, at))
                    arrays.append(p)
                at += n
                scales.append(set_scale)
                wants.append(set_wanted)
            tiles.append(tile)
        width = min(256, far_cols)
        plan, heads, bases = [], [], []
        for g in chosen:
            one, two, base, pair = groups[g]
            blocks = one.shape[1] // width
            plan.append((len(heads), len(heads) + 1, blocks))
            heads += [one, two]
            for k in range(blocks):
                bases += [base + k * width, pair + k * width]
        return stats(
            tiles,
            at,
            plan,
            kofs,
            jnp.stack(bases).astype(jnp.int32),
            jnp.concatenate(scales),
            jnp.concatenate(wants),
            arrays,
            heads,
        )

    set_a = (a_pieces, scale[:cut], wanted[:cut])
    set_b = (b_pieces, scale[cut:], wanted[cut:])
    set_ya = (ya_pieces, y_scale[:cut], y_wanted[:cut])
    set_yb = (yb_pieces, y_scale[cut:], y_wanted[cut:])
    last = n_far
    early = list(range(0, max(1, last - 1)))
    late = list(range(max(1, last - 1), last))
    parts_a = [call([[set_a]], early)]
    if late:
        parts_a.append(call([[set_a]], late))
    parts_ya = [call([[set_ya]], early + late)]
    both = call([[set_b, set_yb]], early + late)
    ends = call([[set_a, set_b], [set_ya, set_yb]], [last])
    own = jnp.concatenate([merge(jnp.stack(parts_a)), both[:, :blk]], axis=1)
    peer = jnp.concatenate([parts_ya[0], both[:, blk:]], axis=1)
    own = merge(jnp.stack([own, ends[:, :half]]))
    peer = merge(jnp.stack([peer, ends[:, half:]]))

    first = q // 2 == 0
    whole = jnp.stack([jnp.where(first, own, peer), jnp.where(first, peer, own)])
    whole = whole.reshape(2, 4, spots, blk).transpose(0, 2, 1, 3).reshape(2 * spots, 4 * blk)
    kin = [
        [(2 * a + b) * n_vocab + 2 * k + core for a in range(2) for k in range(spots)]
        for b in range(2)
        for core in range(2)
    ]
    whole = lax.all_to_all(
        whole, every, split_axis=0, concat_axis=0, axis_index_groups=kin, tiled=True
    )
    peak, total, moment, picked = merge(whole.reshape(2 * spots, 4, blk))
    log_total = peak + jnp.log(total)
    lp, ent = picked - log_total, log_total - moment / total

    seq_lens = lengths[0, :-1]
    stops = jnp.cumsum(seq_lens)
    starts = stops - seq_lens
    local = v * blk + jnp.arange(blk, dtype=jnp.int32)
    valid = local < stops[-1]
    lp = jnp.where(valid, lp, 0.0)
    ent = jnp.where(valid, ent, 0.0)
    member = (local[None, :] >= starts[:, None]) & (local[None, :] < stops[:, None])
    sums = jnp.sum(jnp.where(member[None], jnp.stack([lp, ent])[:, None, :], 0.0), axis=2)
    sums = jnp.sum(
        lax.all_to_all(
            jnp.broadcast_to(sums.reshape(1, -1), (n_vocab, sums.size)),
            "vocab",
            split_axis=0,
            concat_axis=0,
            tiled=True,
        ),
        axis=0,
    ).reshape(sums.shape)
    means = sums / seq_lens.astype(jnp.float32)[None]
    return (lp, ent, means[0], means[1])


def solution(mesh):
    in_specs = (P("req", "vocab"), P(), P(None, ("req", "vocab")), P("req"), P("req", None))
    out_specs = (P(("req", "vocab")), P(("req", "vocab")), P("req"), P("req"))
    return jax.shard_map(shards, mesh=mesh, in_specs=in_specs, out_specs=out_specs, check_vma=False)
```

```python
import functools
import jax
import jax.numpy as jnp
from jax import lax
from jax.experimental import pallas as pl
from jax.experimental.pallas import tpu as pltpu
from jax.sharding import PartitionSpec as P


def stats_kernel(tiles, n_pieces, n_heads, *refs):
    kofs, colbase, side_ref = refs[:3]
    pieces = refs[3 : 3 + n_pieces]
    heads = refs[3 + n_pieces : 3 + n_pieces + n_heads]
    out_ref, x_scr, h_scr, f_scr, t_scr, m_scr, s_scr, w_scr, p_scr, x_sem, h_sem = refs[
        3 + n_pieces + n_heads :
    ]
    step = pl.program_id(0)
    n_tiles, width = len(tiles), h_scr.shape[3]
    firsts = [0]
    for _, columns in tiles:
        firsts.append(firsts[-1] + sum(g[2] for g in columns))
    slot = lax.rem(step, 2)

    def depth_at(j, size):
        return pl.multiple_of(kofs[j], 128) if j >= 0 else (-1 - j) * size

    def row_copies(k):
        return [
            pltpu.make_async_copy(
                pieces[a].at[pl.ds(src, rows)],
                x_scr.at[k % 2, pl.ds(dst, rows), pl.ds(depth_at(j, pieces[a].shape[1]), pieces[a].shape[1])],
                x_sem.at[k % 2],
            )
            for a, j, src, rows, dst in tiles[k][0]
        ]

    def head_copies(parts, block, slot):
        return [
            pltpu.make_async_copy(
                heads[k].at[:, pl.ds(pl.multiple_of(block * width, width), width)],
                h_scr.at[slot, which, pl.ds(n * heads[k].shape[0], heads[k].shape[0])],
                h_sem.at[slot],
            )
            for which in range(2)
            for n, k in enumerate(parts[which])
        ]

    def start_head(at, slot):
        first = 0
        for _, columns in tiles:
            for one, two, blocks in columns:
                @pl.when((at >= first) & (at < first + blocks))
                def _(parts=(one, two), first=first):
                    for copy in head_copies(parts, at - first, slot):
                        copy.start()
                first += blocks

    @pl.when(step == 0)
    def _():
        for copy in row_copies(0):
            copy.start()
        start_head(0, 0)

    for k in range(n_tiles):
        @pl.when(step == firsts[k])
        def _(k=k):
            if k + 1 < n_tiles:
                for copy in row_copies(k + 1):
                    copy.start()
            rows = x_scr.shape[1]
            f_scr[...] = jnp.broadcast_to(side_ref[0:1, :], (128, rows)).T
            lane = lax.broadcasted_iota(jnp.int32, (rows, 128), 1)
            t_scr[...] = jnp.broadcast_to(side_ref[1:2, :], (128, rows)).T.astype(jnp.int32) - lane
            m_scr[...] = jnp.full(m_scr.shape, -jnp.inf, jnp.float32)
            s_scr[...] = jnp.zeros(s_scr.shape, jnp.float32)
            w_scr[...] = jnp.zeros(w_scr.shape, jnp.float32)
            p_scr[...] = jnp.zeros(p_scr.shape, jnp.float32)
            for copy in row_copies(k):
                copy.wait()

    @pl.when(step + 1 < firsts[-1])
    def _():
        start_head(step + 1, lax.rem(step + 1, 2))

    for copy in head_copies(tiles[0][1][0], 0, slot):
        copy.wait()

    held = sum(((step >= f).astype(jnp.int32) for f in firsts[1:-1]), jnp.int32(0))
    rows, sub = x_scr.shape[1], 64

    for which in range(2):
        raw = jnp.dot(x_scr[lax.rem(held, 2)], h_scr[slot, which], preferred_element_type=jnp.float32)
        base = colbase[step * 2 + which]
        for at in range(0, rows, sub):
            here = pl.ds(at, sub)
            scale = f_scr[here, :]
            wanted = t_scr[here, :] - base
            parts = [raw[at : at + sub, c : c + 128] * scale for c in range(0, width, 128)]
            old = m_scr[here, :]
            new = functools.reduce(jnp.maximum, parts, old)
            fade = jnp.exp(old - new)
            total, moment, picked = s_scr[here, :] * fade, w_scr[here, :] * fade, p_scr[here, :]
            for c, part in enumerate(parts):
                weight = jnp.exp(part - new)
                total += weight
                moment += weight * part
                picked = jnp.where(wanted == c * 128, part, picked)
            m_scr[here, :], s_scr[here, :], w_scr[here, :], p_scr[here, :] = new, total, moment, picked

    for last in firsts[1:]:
        @pl.when(step == last - 1)
        def _():
            peak_t = m_scr[...].T
            peak = jnp.max(peak_t, axis=0, keepdims=True)
            fade = jnp.exp(peak_t - peak)
            out_ref[0:1, :] = peak
            out_ref[1:2, :] = jnp.sum(s_scr[...].T * fade, axis=0, keepdims=True)
            out_ref[2:3, :] = jnp.sum(w_scr[...].T * fade, axis=0, keepdims=True)
            out_ref[3:4, :] = jnp.sum(p_scr[...].T, axis=0, keepdims=True)


def stats(tiles, rows, width, kofs, colbase, side, pieces, heads):
    n_tiles = len(tiles)
    counts = [sum(g[2] for g in columns) for _, columns in tiles]
    firsts = [sum(counts[:k]) for k in range(1, n_tiles)]
    n_steps, depth = sum(counts), heads[0].shape[0]

    def block(step):
        return 0, sum(((step >= f).astype(jnp.int32) for f in firsts), jnp.int32(0))

    return pl.pallas_call(
        functools.partial(stats_kernel, tiles, len(pieces), len(heads)),
        grid=(n_steps,),
        in_specs=[pl.BlockSpec(memory_space=pltpu.SMEM)] * 2
        + [pl.BlockSpec((2, rows), block)]
        + [pl.BlockSpec(memory_space=pl.ANY)] * (len(pieces) + len(heads)),
        out_specs=pl.BlockSpec((4, rows), block),
        out_shape=jax.ShapeDtypeStruct((4, n_tiles * rows), jnp.float32),
        scratch_shapes=[
            pltpu.VMEM((min(n_tiles, 2), rows, depth), jnp.bfloat16),
            pltpu.VMEM((2, 2, depth, width), jnp.bfloat16),
        ]
        + [pltpu.VMEM((rows, 128), jnp.float32), pltpu.VMEM((rows, 128), jnp.int32)]
        + [pltpu.VMEM((rows, 128), jnp.float32)] * 4
        + [pltpu.SemaphoreType.DMA((min(n_tiles, 2),)), pltpu.SemaphoreType.DMA((2,))],
        compiler_params=pltpu.CompilerParams(
            dimension_semantics=("arbitrary",), vmem_limit_bytes=48 * 1024 * 1024
        ),
        cost_estimate=pl.CostEstimate(flops=1 << 20, bytes_accessed=1 << 10, transcendentals=0),
    )(kofs, colbase, side, *pieces, *heads)


EPS = 1e-05
SHRINK = 2.0**-9


def merge(stats):
    peak, total, moment, picked = (stats[:, k] for k in range(4))
    best = jnp.max(peak, axis=0)
    fade = jnp.exp(peak - best[None])
    return jnp.stack(
        [best, jnp.sum(total * fade, axis=0), jnp.sum(moment * fade, axis=0), jnp.sum(picked, axis=0)]
    )


def shards(hidden, gain, head, targets, lengths):
    n_req, n_vocab = lax.axis_size("req"), lax.axis_size("vocab")
    q, v = lax.axis_index("req"), lax.axis_index("vocab")
    spots = n_vocab // 2
    s, c = v // 2, v % 2
    rows, feats = hidden.shape
    depth, cols = head.shape
    blk, half = rows // n_vocab, rows // 2
    cut = half - blk
    every = ("req", "vocab")

    def move(x, where):
        pairs = [
            (a * n_vocab + b, where(a, b)) for a in range(n_req) for b in range(n_vocab)
        ]
        return lax.ppermute(x, every, pairs)

    def to_core(x):
        return move(x, lambda a, b: a * n_vocab + (b ^ 1))

    def to_x(x):
        return move(x, lambda a, b: (a ^ 1) * n_vocab + b)

    def to_y(x):
        return move(x, lambda a, b: (a ^ 2) * n_vocab + b)

    def to_z(x, by):
        return move(x, lambda a, b: a * n_vocab + (b + 2 * by) % n_vocab)

    n_far = 4 if cols % 512 == 0 else 1
    far_cols = cols // n_far
    width = min(256, far_cols)

    values = hidden.astype(jnp.float32)
    own_gain = lax.dynamic_slice_in_dim(gain, v * feats, feats) * SHRINK
    scaled = (values * own_gain[None, :]).astype(jnp.bfloat16).reshape(spots, 2, blk, feats)
    square = jnp.sum(values * values, axis=1).reshape(spots, 2, blk)

    def mine(x, core):
        x = lax.dynamic_index_in_dim(x, core, 1, keepdims=False)
        return x.reshape(half, *x.shape[2:])

    token = [None]

    def after(x):
        return x if token[0] is None else lax.optimization_barrier((x, token[0]))[0]

    def step_ends(*results):
        one = results[0][:1, :1].astype(jnp.float32) if token[0] is None else token[0]
        token[0] = lax.optimization_barrier((one, *results))[0]

    def far_part(k):
        return after(head)[:, k * far_cols : (k + 1) * far_cols]

    far = [to_x(far_part(0))]
    other = to_core(mine(scaled, 1 - c))
    other_square = to_core(mine(square, 1 - c).reshape(1, half))
    square_sum = other_square + mine(square, c).reshape(1, half)
    one = mine(scaled, c)
    piece = jnp.where(
        c == 0, jnp.concatenate([one, other], axis=1), jnp.concatenate([other, one], axis=1)
    )
    n_a = half // 2
    a, b = {0: (piece, 0)}, {0: (piece, n_a)}
    ya, yb, far_near = {}, {}, []
    step_ends(other, other_square)
    near = to_core(after(head))

    trip = [0] + [j for k in range(1, spots // 2 + 1) for j in dict.fromkeys((k, spots - k))]
    z_list = [(ring, j) for ring in (a, b) for j in trip[1:]]
    y_list = [(a, ya, 0), (b, yb, 0)] + [(ring, out, j) for ring, out in ((a, ya), (b, yb)) for j in trip[1:]]
    stage = max(1, len(y_list) // 4)
    doubled = 0
    side = y_side = None
    kofs = (s + spots - jnp.arange(spots, dtype=jnp.int32)) % spots * (2 * feats)

    def group(g):
        if g == 0:
            return head, near, (q * n_vocab + v) * cols, (q * n_vocab + (v ^ 1)) * cols
        at = (g - 1) * far_cols
        return (
            far[g - 1],
            far_near[g - 1],
            ((q ^ 1) * n_vocab + v) * cols + at,
            ((q ^ 1) * n_vocab + (v ^ 1)) * cols + at,
        )

    def call(*wanted):
        tiles, arrays, heads, sides, bases, places = [], [], [], [], [], {}
        for name, chosen in wanted:
            ring = {"A": a, "B": b, "E": ya, "F": yb}[name]
            at = n_a if name in "BF" else 0
            sides.append((side if name in "AB" else y_side)[:, at : at + n_a])
            rows = []
            for j in trip:
                key = next((k for k, x in enumerate(arrays) if x is ring[j][0]), len(arrays))
                places[name, j] = key
                if key == len(arrays):
                    arrays.append(ring[j][0])
                rows.append((places[name, j], j, ring[j][1], n_a, 0))
            columns = []
            for g in chosen:
                one, two, base, pair = group(g)
                for key, array in ((("h", g, 0), one), (("h", g, 1), two)):
                    places.setdefault(key, len(heads))
                    if places[key] == len(heads):
                        heads.append(array)
                blocks = one.shape[1] // width
                columns.append(([places["h", g, 0]], [places["h", g, 1]], blocks))
                for k in range(blocks):
                    bases += [base + k * width, pair + k * width]
            tiles.append((rows, columns))
        out = stats(
            tiles,
            n_a,
            width,
            kofs,
            jnp.stack(bases).astype(jnp.int32),
            after(jnp.concatenate(sides, axis=1)),
            arrays,
            heads,
        )
        for k, (name, _) in enumerate(wanted):
            outs[name].append(out[:, k * n_a : (k + 1) * n_a])
        return out

    outs = {name: [] for name in "ABEF"}
    n_steps = 4
    tiny = square_sum
    for step in range(n_steps):
        ends = []
        if 1 <= step and step + 1 < n_far:
            far.append(to_x(far_part(step + 1)))
        if step and step <= n_far:
            far_near.append(to_core(after(far[step - 1])))
        for n in range(len(z_list) if step == n_steps - 2 else min(stage, len(z_list))):
            ring, j = z_list.pop(0)
            by = 1 if j <= spots // 2 else -1
            array, at = ring[(j - by) % spots]
            array = after(array[at : at + n_a])
            if step == 0 and n == 1:
                array = lax.optimization_barrier((array, near))[0]
            ring[j] = (to_z(array, by), 0)
            ends.append(ring[j][0])
            if step == 0 and n == 0 and n_far > 1:
                block = lax.optimization_barrier((head, ends[0]))[0]
                far.append(to_x(block[:, far_cols : 2 * far_cols]))
        batch = [y_list.pop(0) for _ in range(len(y_list) if step == n_steps - 1 else min(stage, len(y_list)))]
        cuts = [[y for y in batch if y[0] is a], [y for y in batch if y[0] is b]] if step == 2 else [batch]
        for part in cuts:
            arrays = [ring[j][0][ring[j][1] : ring[j][1] + n_a] for ring, _, j in part]
            sent = to_y(after(piece if step == 0 and len(part) == 2 else jnp.concatenate(arrays)))
            for n, (_, out, j) in enumerate(part):
                out[j] = (sent, n * n_a)
            ends.append(sent)
        for _ in range(1 if spots == 4 else 5):
            if 2**doubled < spots:
                sent = to_z(after(tiny), 2**doubled)
                tiny = tiny + sent
                doubled += 1
                ends.append(sent)
        if step == 2:
            scale = lax.rsqrt(tiny / depth + EPS) * (1.0 / SHRINK)
            wanted = mine(targets.astype(jnp.float32).reshape(spots, 2, blk), c).reshape(1, half)
            side = jnp.concatenate([scale, wanted])
            y_side = to_y(after(side))
            ends.append(y_side)
        if step == 2:
            many = n_far > 1
            first = call(("A", [0, 1, 2] if many else [0]))
            y_side = lax.optimization_barrier((y_side, first))[0]
            ends.append(call(("E", [0, 1] if many else [0])))
        if step == 3:
            more = [("E", [2, 3]), ("A", [3])] if many else []
            ends.append(call(("B", [0, 1, 2, 3] if many else [0]), *more))
        ends.append(far[min(step, n_far - 1)])
        if step == 0:
            ends.append(near)
        step_ends(*ends)
    if n_far > 3:
        far_near.append(to_core(after(far[3])))
    call(("F", list(range(n_far + 1))), ("A", [n_far]), ("B", [n_far]), ("E", [n_far]))
    own = jnp.concatenate([merge(jnp.stack(outs["A"])), merge(jnp.stack(outs["B"]))], axis=1)
    peer = jnp.concatenate([merge(jnp.stack(outs["E"])), outs["F"][0]], axis=1)

    first = q // 2 == 0
    whole = jnp.stack([jnp.where(first, own, peer), jnp.where(first, peer, own)])
    whole = whole.reshape(2, 4, spots, blk).transpose(0, 2, 1, 3).reshape(2 * spots, 4 * blk)
    kin = [
        [(2 * a + b) * n_vocab + 2 * k + core for a in range(2) for k in range(spots)]
        for b in range(2)
        for core in range(2)
    ]
    whole = lax.all_to_all(
        whole, every, split_axis=0, concat_axis=0, axis_index_groups=kin, tiled=True
    )
    peak, total, moment, picked = merge(whole.reshape(2 * spots, 4, blk))
    log_total = peak + jnp.log(total)
    lp, ent = picked - log_total, log_total - moment / total

    seq_lens = lengths[0, :-1]
    stops = jnp.cumsum(seq_lens)
    starts = stops - seq_lens
    local = v * blk + jnp.arange(blk, dtype=jnp.int32)
    valid = local < stops[-1]
    lp = jnp.where(valid, lp, 0.0)
    ent = jnp.where(valid, ent, 0.0)
    member = (local[None, :] >= starts[:, None]) & (local[None, :] < stops[:, None])
    sums = jnp.sum(jnp.where(member[None], jnp.stack([lp, ent])[:, None, :], 0.0), axis=2)
    sums = jnp.sum(
        lax.all_to_all(
            jnp.broadcast_to(sums.reshape(1, -1), (n_vocab, sums.size)),
            "vocab",
            split_axis=0,
            concat_axis=0,
            tiled=True,
        ),
        axis=0,
    ).reshape(sums.shape)
    means = sums / seq_lens.astype(jnp.float32)[None]
    return (lp, ent, means[0], means[1])


def solution(mesh):
    in_specs = (P("req", "vocab"), P(), P(None, ("req", "vocab")), P("req"), P("req", None))
    out_specs = (P(("req", "vocab")), P(("req", "vocab")), P("req"), P("req"))
    return jax.shard_map(shards, mesh=mesh, in_specs=in_specs, out_specs=out_specs, check_vma=False)
```

```python
import functools
import jax
import jax.numpy as jnp
from jax import lax
from jax.experimental import pallas as pl
from jax.experimental.pallas import tpu as pltpu
from jax.sharding import PartitionSpec as P


def stats_kernel(tiles, n_pieces, n_heads, *refs):
    kofs, colbase, side_ref = refs[:3]
    pieces = refs[3 : 3 + n_pieces]
    heads = refs[3 + n_pieces : 3 + n_pieces + n_heads]
    out_ref, x_scr, h_scr, f_scr, t_scr, m_scr, s_scr, w_scr, p_scr, x_sem, h_sem = refs[
        3 + n_pieces + n_heads :
    ]
    step = pl.program_id(0)
    n_tiles, width = len(tiles), h_scr.shape[3]
    firsts = [0]
    for _, columns in tiles:
        firsts.append(firsts[-1] + sum(g[2] for g in columns))
    blocks = [(g[0][0], k) for _, columns in tiles for g in columns for k in range(g[2])]
    same = [k for k in range(1, len(blocks)) if blocks[k] == blocks[k - 1]]

    def is_one_of(at, steps):
        return functools.reduce(jnp.logical_or, [at == k for k in steps], at < 0)

    def slot_of(at):
        return lax.rem(at - sum(((at >= k).astype(jnp.int32) for k in same), jnp.int32(0)), 2)

    slot = slot_of(step)

    def depth_at(j, size):
        return pl.multiple_of(kofs[j], 128) if j >= 0 else (-1 - j) * size

    def row_copies(k):
        return [
            pltpu.make_async_copy(
                pieces[a].at[pl.ds(src, rows)],
                x_scr.at[k % 2, pl.ds(dst, rows), pl.ds(depth_at(j, pieces[a].shape[1]), pieces[a].shape[1])],
                x_sem.at[k % 2],
            )
            for a, j, src, rows, dst in tiles[k][0]
        ]

    def head_copies(parts, block, slot):
        return [
            pltpu.make_async_copy(
                heads[k].at[:, pl.ds(pl.multiple_of(block * width, width), width)],
                h_scr.at[slot, which, pl.ds(n * heads[k].shape[0], heads[k].shape[0])],
                h_sem.at[slot],
            )
            for which in range(2)
            for n, k in enumerate(parts[which])
        ]

    def start_head(at, slot):
        first = 0
        for _, columns in tiles:
            for one, two, blocks in columns:
                @pl.when((at >= first) & (at < first + blocks))
                def _(parts=(one, two), first=first):
                    for copy in head_copies(parts, at - first, slot):
                        copy.start()
                first += blocks

    @pl.when(step == 0)
    def _():
        for copy in row_copies(0):
            copy.start()
        start_head(0, 0)

    for k in range(n_tiles):
        @pl.when(step == firsts[k])
        def _(k=k):
            if k + 1 < n_tiles:
                for copy in row_copies(k + 1):
                    copy.start()
            rows = x_scr.shape[1]
            f_scr[...] = jnp.broadcast_to(side_ref[0:1, :], (128, rows)).T
            lane = lax.broadcasted_iota(jnp.int32, (rows, 128), 1)
            t_scr[...] = jnp.broadcast_to(side_ref[1:2, :], (128, rows)).T.astype(jnp.int32) - lane
            m_scr[...] = jnp.full(m_scr.shape, -jnp.inf, jnp.float32)
            s_scr[...] = jnp.zeros(s_scr.shape, jnp.float32)
            w_scr[...] = jnp.zeros(w_scr.shape, jnp.float32)
            p_scr[...] = jnp.zeros(p_scr.shape, jnp.float32)
            for copy in row_copies(k):
                copy.wait()

    @pl.when((step + 1 < firsts[-1]) & jnp.logical_not(is_one_of(step + 1, same)))
    def _():
        start_head(step + 1, slot_of(step + 1))

    @pl.when(jnp.logical_not(is_one_of(step, same)))
    def _():
        for copy in head_copies(tiles[0][1][0], 0, slot):
            copy.wait()

    held = sum(((step >= f).astype(jnp.int32) for f in firsts[1:-1]), jnp.int32(0))
    rows, sub = x_scr.shape[1], 64

    raws = [
        jnp.dot(x_scr[lax.rem(held, 2)], h_scr[slot, which], preferred_element_type=jnp.float32)
        for which in range(2)
    ]
    bases = [colbase[step * 2 + which] + c for which in range(2) for c in range(0, width, 128)]
    for at in range(0, rows, sub):
        here = pl.ds(at, sub)
        scale, wanted = f_scr[here, :], t_scr[here, :]
        parts = [raw[at : at + sub, c : c + 128] * scale for raw in raws for c in range(0, width, 128)]
        old = m_scr[here, :]
        new = functools.reduce(jnp.maximum, parts, old)
        fade = jnp.exp(old - new)
        total, moment, picked = s_scr[here, :] * fade, w_scr[here, :] * fade, p_scr[here, :]
        for base, part in zip(bases, parts):
            weight = jnp.exp(part - new)
            total += weight
            moment += weight * part
            picked = jnp.where(wanted == base, part, picked)
        m_scr[here, :], s_scr[here, :], w_scr[here, :], p_scr[here, :] = new, total, moment, picked

    for last in firsts[1:]:
        @pl.when(step == last - 1)
        def _():
            peak_t = m_scr[...].T
            peak = jnp.max(peak_t, axis=0, keepdims=True)
            fade = jnp.exp(peak_t - peak)
            out_ref[0:1, :] = peak
            out_ref[1:2, :] = jnp.sum(s_scr[...].T * fade, axis=0, keepdims=True)
            out_ref[2:3, :] = jnp.sum(w_scr[...].T * fade, axis=0, keepdims=True)
            out_ref[3:4, :] = jnp.sum(p_scr[...].T, axis=0, keepdims=True)


def stats(tiles, rows, width, kofs, colbase, side, pieces, heads):
    n_tiles = len(tiles)
    counts = [sum(g[2] for g in columns) for _, columns in tiles]
    firsts = [sum(counts[:k]) for k in range(1, n_tiles)]
    n_steps, depth = sum(counts), heads[0].shape[0]

    def block(step):
        return 0, sum(((step >= f).astype(jnp.int32) for f in firsts), jnp.int32(0))

    return pl.pallas_call(
        functools.partial(stats_kernel, tiles, len(pieces), len(heads)),
        grid=(n_steps,),
        in_specs=[pl.BlockSpec(memory_space=pltpu.SMEM)] * 2
        + [pl.BlockSpec((2, rows), block)]
        + [pl.BlockSpec(memory_space=pl.ANY)] * (len(pieces) + len(heads)),
        out_specs=pl.BlockSpec((4, rows), block),
        out_shape=jax.ShapeDtypeStruct((4, n_tiles * rows), jnp.float32),
        scratch_shapes=[
            pltpu.VMEM((min(n_tiles, 2), rows, depth), jnp.bfloat16),
            pltpu.VMEM((2, 2, depth, width), jnp.bfloat16),
        ]
        + [pltpu.VMEM((rows, 128), jnp.float32), pltpu.VMEM((rows, 128), jnp.int32)]
        + [pltpu.VMEM((rows, 128), jnp.float32)] * 4
        + [pltpu.SemaphoreType.DMA((min(n_tiles, 2),)), pltpu.SemaphoreType.DMA((2,))],
        compiler_params=pltpu.CompilerParams(
            dimension_semantics=("arbitrary",), vmem_limit_bytes=48 * 1024 * 1024
        ),
        cost_estimate=pl.CostEstimate(flops=1 << 20, bytes_accessed=1 << 10, transcendentals=0),
    )(kofs, colbase, side, *pieces, *heads)


EPS = 1e-05
SHRINK = 2.0**-9


def merge(stats):
    peak, total, moment, picked = (stats[:, k] for k in range(4))
    best = jnp.max(peak, axis=0)
    fade = jnp.exp(peak - best[None])
    return jnp.stack(
        [best, jnp.sum(total * fade, axis=0), jnp.sum(moment * fade, axis=0), jnp.sum(picked, axis=0)]
    )


def shards(hidden, gain, head, targets, lengths):
    n_req, n_vocab = lax.axis_size("req"), lax.axis_size("vocab")
    q, v = lax.axis_index("req"), lax.axis_index("vocab")
    spots = n_vocab // 2
    s, c = v // 2, v % 2
    rows, feats = hidden.shape
    depth, cols = head.shape
    blk, half = rows // n_vocab, rows // 2
    cut = half - blk
    every = ("req", "vocab")

    def move(x, where):
        pairs = [
            (a * n_vocab + b, where(a, b)) for a in range(n_req) for b in range(n_vocab)
        ]
        return lax.ppermute(x, every, pairs)

    def to_core(x):
        return move(x, lambda a, b: a * n_vocab + (b ^ 1))

    def to_x(x):
        return move(x, lambda a, b: (a ^ 1) * n_vocab + b)

    def to_y(x):
        return move(x, lambda a, b: (a ^ 2) * n_vocab + b)

    def to_z(x, by):
        return move(x, lambda a, b: a * n_vocab + (b + 2 * by) % n_vocab)

    n_far = 4 if cols % 512 == 0 else 1
    far_cols = cols // n_far
    width = min(256, far_cols)

    values = hidden.astype(jnp.float32)
    own_gain = lax.dynamic_slice_in_dim(gain, v * feats, feats) * SHRINK
    scaled = (values * own_gain[None, :]).astype(jnp.bfloat16).reshape(spots, 2, blk, feats)
    square = jnp.sum(values * values, axis=1).reshape(spots, 2, blk)

    def mine(x, core):
        x = lax.dynamic_index_in_dim(x, core, 1, keepdims=False)
        return x.reshape(half, *x.shape[2:])

    token = [None]

    def after(x):
        return x if token[0] is None else lax.optimization_barrier((x, token[0]))[0]

    def step_ends(*results):
        one = results[0][:1, :1].astype(jnp.float32) if token[0] is None else token[0]
        token[0] = lax.optimization_barrier((one, *results))[0]

    blocks = [head[:, :far_cols]]

    def far_part(k):
        return after(blocks[k])

    far = [to_x(far_part(0))]
    other = to_core(mine(scaled, 1 - c))
    other_square = to_core(mine(square, 1 - c).reshape(1, half))
    square_sum = other_square + mine(square, c).reshape(1, half)
    one = mine(scaled, c)
    piece = jnp.where(
        c == 0, jnp.concatenate([one, other], axis=1), jnp.concatenate([other, one], axis=1)
    )
    n_a = half // 2
    a, b = {0: (piece, 0)}, {0: (piece, n_a)}
    ya, yb, far_near = {}, {}, []
    step_ends(other, other_square)
    near = to_core(after(head))

    trip = [0] + [j for k in range(1, spots // 2 + 1) for j in dict.fromkeys((k, spots - k))]
    z_list = [(ring, j) for ring in (a, b) for j in trip[1:]]
    y_list = [(a, ya, 0), (b, yb, 0)] + [(ring, out, j) for ring, out in ((a, ya), (b, yb)) for j in trip[1:]]
    stage = max(1, len(y_list) // 4)
    doubled = 0
    side = y_side = None
    kofs = (s + spots - jnp.arange(spots, dtype=jnp.int32)) % spots * (2 * feats)

    def group(g):
        if g == 0:
            return head, near, (q * n_vocab + v) * cols, (q * n_vocab + (v ^ 1)) * cols
        at = (g - 1) * far_cols
        return (
            far[g - 1],
            far_near[g - 1],
            ((q ^ 1) * n_vocab + v) * cols + at,
            ((q ^ 1) * n_vocab + (v ^ 1)) * cols + at,
        )

    def call(*wanted):
        tiles, arrays, heads, sides, bases, places = [], [], [], [], [], {}
        for name, chosen in wanted:
            ring = {"A": a, "B": b, "E": ya, "F": yb}[name]
            at = n_a if name in "BF" else 0
            sides.append((side if name in "AB" else y_side)[:, at : at + n_a])
            rows = []
            for j in trip:
                key = next((k for k, x in enumerate(arrays) if x is ring[j][0]), len(arrays))
                places[name, j] = key
                if key == len(arrays):
                    arrays.append(ring[j][0])
                rows.append((places[name, j], j, ring[j][1], n_a, 0))
            columns = []
            for g in chosen:
                one, two, base, pair = group(g)
                for key, array in ((("h", g, 0), one), (("h", g, 1), two)):
                    places.setdefault(key, len(heads))
                    if places[key] == len(heads):
                        heads.append(array)
                blocks = one.shape[1] // width
                columns.append(([places["h", g, 0]], [places["h", g, 1]], blocks))
                for k in range(blocks):
                    bases += [base + k * width, pair + k * width]
            tiles.append((rows, columns))
        out = stats(
            tiles,
            n_a,
            width,
            kofs,
            jnp.stack(bases).astype(jnp.int32),
            after(jnp.concatenate(sides, axis=1)),
            arrays,
            heads,
        )
        for k, (name, _) in enumerate(wanted):
            outs[name].append(out[:, k * n_a : (k + 1) * n_a])
        return out

    outs = {name: [] for name in "ABEF"}
    n_steps = 4
    tiny = square_sum
    for step in range(n_steps):
        ends = []
        if 1 <= step and step + 1 < n_far:
            far.append(to_x(far_part(step + 1)))
        if step and step <= n_far:
            far_near.append(to_core(after(far[step - 1])))
        for n in range(len(z_list) if step == n_steps - 2 else min(stage, len(z_list))):
            ring, j = z_list.pop(0)
            by = 1 if j <= spots // 2 else -1
            array, at = ring[(j - by) % spots]
            array = after(array[at : at + n_a])
            if step == 0 and n == 1:
                array = lax.optimization_barrier((array, near))[0]
            ring[j] = (to_z(array, by), 0)
            ends.append(ring[j][0])
            if step == 0 and n == 0 and n_far > 1:
                rest = lax.optimization_barrier((head, ends[0]))[0]
                blocks += [rest[:, k * far_cols : (k + 1) * far_cols] for k in range(1, n_far)]
                far.append(to_x(blocks[1]))
                ends += blocks[1:]
        if step == n_steps - 1:
            for _, out, j in [y for y in y_list if y[2] > spots // 2]:
                array, at = out[(j + 1) % spots]
                out[j] = (to_z(after(array[at : at + n_a]), -1), 0)
                ends.append(out[j][0])
            y_list = [y for y in y_list if y[2] <= spots // 2]
        batch = [y_list.pop(0) for _ in range(len(y_list) if step == n_steps - 1 else min(stage, len(y_list)))]
        cuts = [[y for y in batch if y[0] is a], [y for y in batch if y[0] is b]] if step == 2 else [batch]
        for part in cuts:
            arrays = [ring[j][0][ring[j][1] : ring[j][1] + n_a] for ring, _, j in part]
            sent = to_y(after(piece if step == 0 and len(part) == 2 else jnp.concatenate(arrays)))
            for n, (_, out, j) in enumerate(part):
                out[j] = (sent, n * n_a)
            ends.append(sent)
        for _ in range(1 if spots == 4 else 5):
            if 2**doubled < spots:
                sent = to_z(after(tiny), 2**doubled)
                tiny = tiny + sent
                doubled += 1
                ends.append(sent)
        if step == 2:
            scale = lax.rsqrt(tiny / depth + EPS) * (1.0 / SHRINK)
            wanted = mine(targets.astype(jnp.float32).reshape(spots, 2, blk), c).reshape(1, half)
            side = jnp.concatenate([scale, wanted])
            y_side = to_y(after(side))
            ends.append(y_side)
        if step == 2:
            many = n_far > 1
            first = call(("A", [0, 1, 2] if many else [0]))
            y_side = lax.optimization_barrier((y_side, first))[0]
            ends.append(call(("E", [0, 1, 2] if many else [0])))
        if step == 3:
            more = [("E", [3]), ("A", [3])] if many else []
            ends.append(call(("B", [0, 1, 2, 3] if many else [0]), *more))
        if step < n_steps - 1:
            ends.append(far[min(step, n_far - 1)])
        if step == 0:
            ends.append(near)
        step_ends(*ends)
    if many:
        ends = call(("F", [0, 1, 2, 3]))
        far_near.append(to_core(lax.optimization_barrier((far[3], ends))[0]))
        y_side = lax.optimization_barrier((y_side, ends))[0]
        call(("F", [4]), ("A", [4]), ("B", [4]), ("E", [4]))
    else:
        call(("F", [0, 1]), ("A", [1]), ("B", [1]), ("E", [1]))
    own = jnp.concatenate([merge(jnp.stack(outs["A"])), merge(jnp.stack(outs["B"]))], axis=1)
    peer = jnp.concatenate([merge(jnp.stack(outs["E"])), merge(jnp.stack(outs["F"]))], axis=1)

    first = q // 2 == 0
    whole = jnp.stack([jnp.where(first, own, peer), jnp.where(first, peer, own)])
    whole = jnp.broadcast_to(whole.reshape(2, 1, 4 * half), (2, spots, 4 * half))
    kin = [
        [(2 * a + b) * n_vocab + 2 * k + core for a in range(2) for k in range(spots)]
        for b in range(2)
        for core in range(2)
    ]
    whole = lax.all_to_all(
        whole.reshape(2 * spots, 4 * half), every, split_axis=0, concat_axis=0, axis_index_groups=kin, tiled=True
    )
    peak, total, moment, picked = merge(whole.reshape(2 * spots, 4, half))
    log_total = peak + jnp.log(total)
    lp, ent = picked - log_total, log_total - moment / total

    seq_lens = lengths[0, :-1]
    stops = jnp.cumsum(seq_lens)
    starts = stops - seq_lens
    local = jnp.arange(half, dtype=jnp.int32)
    local = (local // blk * 2 + c) * blk + local % blk
    valid = local < stops[-1]
    lp = jnp.where(valid, lp, 0.0)
    ent = jnp.where(valid, ent, 0.0)
    member = (local[None, :] >= starts[:, None]) & (local[None, :] < stops[:, None])
    sums = jnp.sum(jnp.where(member[None], jnp.stack([lp, ent])[:, None, :], 0.0), axis=2)
    sums = sums + to_core(sums)
    lp = lax.dynamic_slice_in_dim(lp, s * blk, blk)
    ent = lax.dynamic_slice_in_dim(ent, s * blk, blk)
    means = sums / seq_lens.astype(jnp.float32)[None]
    return (lp, ent, means[0], means[1])


def solution(mesh):
    in_specs = (P("req", "vocab"), P(), P(None, ("req", "vocab")), P("req"), P("req", None))
    out_specs = (P(("req", "vocab")), P(("req", "vocab")), P("req"), P("req"))
    return jax.shard_map(shards, mesh=mesh, in_specs=in_specs, out_specs=out_specs, check_vma=False)
```

```python
import functools
import jax
import jax.numpy as jnp
from jax import lax
from jax.experimental import pallas as pl
from jax.experimental.pallas import tpu as pltpu
from jax.sharding import PartitionSpec as P


def stats_kernel(tiles, n_pieces, n_heads, *refs):
    kofs, colbase, side_ref = refs[:3]
    pieces = refs[3 : 3 + n_pieces]
    heads = refs[3 + n_pieces : 3 + n_pieces + n_heads]
    out_ref, x_scr, h_scr, f_scr, t_scr, m_scr, s_scr, w_scr, p_scr, x_sem, h_sem = refs[
        3 + n_pieces + n_heads :
    ]
    step = pl.program_id(0)
    n_tiles, width = len(tiles), h_scr.shape[3]
    firsts = [0]
    for _, columns in tiles:
        firsts.append(firsts[-1] + sum(g[2] for g in columns))
    blocks = [(g[0][0], k) for _, columns in tiles for g in columns for k in range(g[2])]
    same = [k for k in range(1, len(blocks)) if blocks[k] == blocks[k - 1]]

    def is_one_of(at, steps):
        return functools.reduce(jnp.logical_or, [at == k for k in steps], at < 0)

    def slot_of(at):
        return lax.rem(at - sum(((at >= k).astype(jnp.int32) for k in same), jnp.int32(0)), 2)

    slot = slot_of(step)

    def depth_at(j, size):
        return pl.multiple_of(kofs[j], 128) if j >= 0 else (-1 - j) * size

    def row_copies(k):
        return [
            pltpu.make_async_copy(
                pieces[a].at[pl.ds(src, rows)],
                x_scr.at[k % 2, pl.ds(dst, rows), pl.ds(depth_at(j, pieces[a].shape[1]), pieces[a].shape[1])],
                x_sem.at[k % 2],
            )
            for a, j, src, rows, dst in tiles[k][0]
        ]

    def head_copies(parts, block, slot):
        return [
            pltpu.make_async_copy(
                heads[k].at[:, pl.ds(pl.multiple_of(block * width, width), width)],
                h_scr.at[slot, which, pl.ds(n * heads[k].shape[0], heads[k].shape[0])],
                h_sem.at[slot],
            )
            for which in range(2)
            for n, k in enumerate(parts[which])
        ]

    def start_head(at, slot):
        first = 0
        for _, columns in tiles:
            for one, two, blocks in columns:
                @pl.when((at >= first) & (at < first + blocks))
                def _(parts=(one, two), first=first):
                    for copy in head_copies(parts, at - first, slot):
                        copy.start()
                first += blocks

    @pl.when(step == 0)
    def _():
        for copy in row_copies(0):
            copy.start()
        start_head(0, 0)

    for k in range(n_tiles):
        @pl.when(step == firsts[k])
        def _(k=k):
            if k + 1 < n_tiles:
                for copy in row_copies(k + 1):
                    copy.start()
            rows = x_scr.shape[1]
            f_scr[...] = jnp.broadcast_to(side_ref[0:1, :], (128, rows)).T
            lane = lax.broadcasted_iota(jnp.int32, (rows, 128), 1)
            t_scr[...] = jnp.broadcast_to(side_ref[1:2, :], (128, rows)).T.astype(jnp.int32) - lane
            m_scr[...] = jnp.full(m_scr.shape, -jnp.inf, jnp.float32)
            s_scr[...] = jnp.zeros(s_scr.shape, jnp.float32)
            w_scr[...] = jnp.zeros(w_scr.shape, jnp.float32)
            p_scr[...] = jnp.zeros(p_scr.shape, jnp.float32)
            for copy in row_copies(k):
                copy.wait()

    @pl.when((step + 1 < firsts[-1]) & jnp.logical_not(is_one_of(step + 1, same)))
    def _():
        start_head(step + 1, slot_of(step + 1))

    @pl.when(jnp.logical_not(is_one_of(step, same)))
    def _():
        for copy in head_copies(tiles[0][1][0], 0, slot):
            copy.wait()

    held = sum(((step >= f).astype(jnp.int32) for f in firsts[1:-1]), jnp.int32(0))
    rows, sub = x_scr.shape[1], 64

    raws = [
        jnp.dot(x_scr[lax.rem(held, 2)], h_scr[slot, which], preferred_element_type=jnp.float32)
        for which in range(2)
    ]
    bases = [colbase[step * 2 + which] + c for which in range(2) for c in range(0, width, 128)]
    for at in range(0, rows, sub):
        here = pl.ds(at, sub)
        scale, wanted = f_scr[here, :], t_scr[here, :]
        parts = [raw[at : at + sub, c : c + 128] * scale for raw in raws for c in range(0, width, 128)]
        old = m_scr[here, :]
        new = functools.reduce(jnp.maximum, parts, old)
        fade = jnp.exp(old - new)
        total, moment, picked = s_scr[here, :] * fade, w_scr[here, :] * fade, p_scr[here, :]
        for base, part in zip(bases, parts):
            weight = jnp.exp(part - new)
            total += weight
            moment += weight * part
            picked = jnp.where(wanted == base, part, picked)
        m_scr[here, :], s_scr[here, :], w_scr[here, :], p_scr[here, :] = new, total, moment, picked

    for last in firsts[1:]:
        @pl.when(step == last - 1)
        def _():
            peak_t = m_scr[...].T
            peak = jnp.max(peak_t, axis=0, keepdims=True)
            fade = jnp.exp(peak_t - peak)
            out_ref[0:1, :] = peak
            out_ref[1:2, :] = jnp.sum(s_scr[...].T * fade, axis=0, keepdims=True)
            out_ref[2:3, :] = jnp.sum(w_scr[...].T * fade, axis=0, keepdims=True)
            out_ref[3:4, :] = jnp.sum(p_scr[...].T, axis=0, keepdims=True)


def stats(tiles, rows, width, kofs, colbase, side, pieces, heads):
    n_tiles = len(tiles)
    counts = [sum(g[2] for g in columns) for _, columns in tiles]
    firsts = [sum(counts[:k]) for k in range(1, n_tiles)]
    n_steps, depth = sum(counts), heads[0].shape[0]

    def block(step):
        return 0, sum(((step >= f).astype(jnp.int32) for f in firsts), jnp.int32(0))

    return pl.pallas_call(
        functools.partial(stats_kernel, tiles, len(pieces), len(heads)),
        grid=(n_steps,),
        in_specs=[pl.BlockSpec(memory_space=pltpu.SMEM)] * 2
        + [pl.BlockSpec((2, rows), block)]
        + [pl.BlockSpec(memory_space=pl.ANY)] * (len(pieces) + len(heads)),
        out_specs=pl.BlockSpec((4, rows), block),
        out_shape=jax.ShapeDtypeStruct((4, n_tiles * rows), jnp.float32),
        scratch_shapes=[
            pltpu.VMEM((min(n_tiles, 2), rows, depth), jnp.bfloat16),
            pltpu.VMEM((2, 2, depth, width), jnp.bfloat16),
        ]
        + [pltpu.VMEM((rows, 128), jnp.float32), pltpu.VMEM((rows, 128), jnp.int32)]
        + [pltpu.VMEM((rows, 128), jnp.float32)] * 4
        + [pltpu.SemaphoreType.DMA((min(n_tiles, 2),)), pltpu.SemaphoreType.DMA((2,))],
        compiler_params=pltpu.CompilerParams(
            dimension_semantics=("arbitrary",), vmem_limit_bytes=48 * 1024 * 1024
        ),
        cost_estimate=pl.CostEstimate(flops=1 << 20, bytes_accessed=1 << 10, transcendentals=0),
    )(kofs, colbase, side, *pieces, *heads)


EPS = 1e-05
SHRINK = 2.0**-9


def merge(stats):
    peak, total, moment, picked = (stats[:, k] for k in range(4))
    best = jnp.max(peak, axis=0)
    fade = jnp.exp(peak - best[None])
    return jnp.stack(
        [best, jnp.sum(total * fade, axis=0), jnp.sum(moment * fade, axis=0), jnp.sum(picked, axis=0)]
    )


def shards(hidden, gain, head, targets, lengths):
    n_req, n_vocab = lax.axis_size("req"), lax.axis_size("vocab")
    q, v = lax.axis_index("req"), lax.axis_index("vocab")
    spots = n_vocab // 2
    s, c = v // 2, v % 2
    rows, feats = hidden.shape
    depth, cols = head.shape
    blk, half = rows // n_vocab, rows // 2
    cut = half - blk
    every = ("req", "vocab")

    def move(x, where):
        pairs = [
            (a * n_vocab + b, where(a, b)) for a in range(n_req) for b in range(n_vocab)
        ]
        return lax.ppermute(x, every, pairs)

    def to_core(x):
        return move(x, lambda a, b: a * n_vocab + (b ^ 1))

    def to_x(x):
        return move(x, lambda a, b: (a ^ 1) * n_vocab + b)

    def to_y(x):
        return move(x, lambda a, b: (a ^ 2) * n_vocab + b)

    def to_z(x, by):
        return move(x, lambda a, b: a * n_vocab + (b + 2 * by) % n_vocab)

    n_far = 4 if cols % 512 == 0 else 1
    far_cols = cols // n_far
    width = min(256, far_cols)

    def mine(x, core):
        x = lax.dynamic_index_in_dim(x, core, 1, keepdims=False)
        return x.reshape(half, *x.shape[2:])

    token = [None]

    def after(x):
        return x if token[0] is None else lax.optimization_barrier((x, token[0]))[0]

    def step_ends(*results):
        one = results[0][:1, :1].astype(jnp.float32) if token[0] is None else token[0]
        token[0] = lax.optimization_barrier((one, *results))[0]

    blocks = [head[:, :far_cols]]

    def far_part(k):
        return after(blocks[k])

    far = [to_x(far_part(0))]
    raw = hidden.reshape(spots, 2, blk, feats)
    other = to_core(mine(raw, 1 - c))
    one = mine(raw, c)
    values = jnp.where(
        c == 0, jnp.concatenate([one, other], axis=1), jnp.concatenate([other, one], axis=1)
    ).astype(jnp.float32)
    pair_gain = lax.dynamic_slice_in_dim(gain, 2 * s * feats, 2 * feats) * SHRINK
    piece = (values * pair_gain[None, :]).astype(jnp.bfloat16)
    square_sum = jnp.sum(values * values, axis=1).reshape(1, half)
    n_a = half // 2
    a, b = {0: (piece, 0)}, {0: (piece, n_a)}
    ya, yb, far_near = {}, {}, []
    step_ends(other)
    near = to_core(after(head))

    trip = [0] + [j for k in range(1, spots // 2 + 1) for j in dict.fromkeys((k, spots - k))]
    z_list = [(ring, j) for ring in (a, b) for j in trip[1:]]
    y_list = [(a, ya, 0), (b, yb, 0)] + [(ring, out, j) for ring, out in ((a, ya), (b, yb)) for j in trip[1:]]
    stage = max(1, len(y_list) // 4)
    doubled = 0
    side = y_side = None
    kofs = (s + spots - jnp.arange(spots, dtype=jnp.int32)) % spots * (2 * feats)

    def group(g):
        if g == 0:
            return head, near, (q * n_vocab + v) * cols, (q * n_vocab + (v ^ 1)) * cols
        at = (g - 1) * far_cols
        return (
            far[g - 1],
            far_near[g - 1],
            ((q ^ 1) * n_vocab + v) * cols + at,
            ((q ^ 1) * n_vocab + (v ^ 1)) * cols + at,
        )

    def call(*wanted):
        tiles, arrays, heads, sides, bases, places = [], [], [], [], [], {}
        for name, chosen in wanted:
            ring = {"A": a, "B": b, "E": ya, "F": yb}[name]
            at = n_a if name in "BF" else 0
            sides.append((side if name in "AB" else y_side)[:, at : at + n_a])
            rows = []
            for j in trip:
                key = next((k for k, x in enumerate(arrays) if x is ring[j][0]), len(arrays))
                places[name, j] = key
                if key == len(arrays):
                    arrays.append(ring[j][0])
                rows.append((places[name, j], j, ring[j][1], n_a, 0))
            columns = []
            for g in chosen:
                one, two, base, pair = group(g)
                for key, array in ((("h", g, 0), one), (("h", g, 1), two)):
                    places.setdefault(key, len(heads))
                    if places[key] == len(heads):
                        heads.append(array)
                blocks = one.shape[1] // width
                columns.append(([places["h", g, 0]], [places["h", g, 1]], blocks))
                for k in range(blocks):
                    bases += [base + k * width, pair + k * width]
            tiles.append((rows, columns))
        out = stats(
            tiles,
            n_a,
            width,
            kofs,
            jnp.stack(bases).astype(jnp.int32),
            after(jnp.concatenate(sides, axis=1)),
            arrays,
            heads,
        )
        for k, (name, _) in enumerate(wanted):
            outs[name].append(out[:, k * n_a : (k + 1) * n_a])
        return out

    outs = {name: [] for name in "ABEF"}
    n_steps = 4
    tiny = square_sum
    for step in range(n_steps):
        ends = []
        if 1 <= step and step + 1 < n_far:
            far.append(to_x(far_part(step + 1)))
        if step and step <= n_far:
            far_near.append(to_core(after(far[step - 1])))
        for n in range(len(z_list) if step == n_steps - 2 else min(stage, len(z_list))):
            ring, j = z_list.pop(0)
            by = 1 if j <= spots // 2 else -1
            array, at = ring[(j - by) % spots]
            array = after(array[at : at + n_a])
            ring[j] = (to_z(array, by), 0)
            ends.append(ring[j][0])
            if step == 0 and n == 0 and n_far > 1:
                rest = lax.optimization_barrier((head, ends[0]))[0]
                blocks += [rest[:, k * far_cols : (k + 1) * far_cols] for k in range(1, n_far)]
                far.append(to_x(blocks[1]))
                ends += blocks[1:]
        if step == n_steps - 1:
            for _, out, j in [y for y in y_list if y[2] > spots // 2]:
                array, at = out[(j + 1) % spots]
                out[j] = (to_z(after(array[at : at + n_a]), -1), 0)
                ends.append(out[j][0])
            y_list = [y for y in y_list if y[2] <= spots // 2]
        batch = [y_list.pop(0) for _ in range(len(y_list) if step == n_steps - 1 else min(stage, len(y_list)))]
        cuts = [[y for y in batch if y[0] is a], [y for y in batch if y[0] is b]] if step == 2 else [batch]
        for part in cuts:
            arrays = [ring[j][0][ring[j][1] : ring[j][1] + n_a] for ring, _, j in part]
            sent = to_y(after(piece if step == 0 and len(part) == 2 else jnp.concatenate(arrays)))
            for n, (_, out, j) in enumerate(part):
                out[j] = (sent, n * n_a)
            ends.append(sent)
        for _ in range(1 if spots == 4 else 5):
            if 2**doubled < spots:
                sent = to_z(lax.optimization_barrier((after(tiny), ends[0]))[0] if step == 0 else after(tiny), 2**doubled)
                tiny = tiny + sent
                doubled += 1
                ends.append(sent)
        if step == 2:
            scale = lax.rsqrt(tiny / depth + EPS) * (1.0 / SHRINK)
            wanted = mine(targets.astype(jnp.float32).reshape(spots, 2, blk), c).reshape(1, half)
            side = jnp.concatenate([scale, wanted])
            y_side = to_y(after(side))
            ends.append(y_side)
        if step == 2:
            many = n_far > 1
            first = call(("A", [0, 1, 2] if many else [0]))
            y_side = lax.optimization_barrier((y_side, first))[0]
            ends.append(call(("E", [0, 1, 2] if many else [0])))
        if step == 3:
            ends.append(call(("B", [0, 1, 2, 3] if many else [0])))
        if step < n_steps - 1:
            ends.append(far[min(step, n_far - 1)])
        if step == 0:
            ends.append(near)
        step_ends(*ends)
    if many:
        ends = call(("F", [0, 1, 2, 3]))
        far_near.append(to_core(lax.optimization_barrier((far[3], ends))[0]))
        y_side = lax.optimization_barrier((y_side, ends))[0]
        ends = call(("E", [3]), ("A", [3]))
        y_side = lax.optimization_barrier((y_side, ends))[0]
        call(("F", [4]), ("A", [4]), ("B", [4]), ("E", [4]))
    else:
        call(("F", [0, 1]), ("A", [1]), ("B", [1]), ("E", [1]))
    own = jnp.concatenate([merge(jnp.stack(outs["A"])), merge(jnp.stack(outs["B"]))], axis=1)
    peer = jnp.concatenate([merge(jnp.stack(outs["E"])), merge(jnp.stack(outs["F"]))], axis=1)

    first = q // 2 == 0
    whole = jnp.stack([jnp.where(first, own, peer), jnp.where(first, peer, own)])
    whole = jnp.broadcast_to(whole.reshape(2, 1, 4 * half), (2, spots, 4 * half))
    kin = [
        [(2 * a + b) * n_vocab + 2 * k + core for a in range(2) for k in range(spots)]
        for b in range(2)
        for core in range(2)
    ]
    whole = lax.all_to_all(
        whole.reshape(2 * spots, 4 * half), every, split_axis=0, concat_axis=0, axis_index_groups=kin, tiled=True
    )
    peak, total, moment, picked = merge(whole.reshape(2 * spots, 4, half))
    log_total = peak + jnp.log(total)
    lp, ent = picked - log_total, log_total - moment / total

    seq_lens = lengths[0, :-1]
    stops = jnp.cumsum(seq_lens)
    starts = stops - seq_lens
    local = jnp.arange(half, dtype=jnp.int32)
    local = (local // blk * 2 + c) * blk + local % blk
    valid = local < stops[-1]
    lp = jnp.where(valid, lp, 0.0)
    ent = jnp.where(valid, ent, 0.0)
    member = (local[None, :] >= starts[:, None]) & (local[None, :] < stops[:, None])
    sums = jnp.sum(jnp.where(member[None], jnp.stack([lp, ent])[:, None, :], 0.0), axis=2)
    sums = sums + to_core(sums)
    lp = lax.dynamic_slice_in_dim(lp, s * blk, blk)
    ent = lax.dynamic_slice_in_dim(ent, s * blk, blk)
    means = sums / seq_lens.astype(jnp.float32)[None]
    return (lp, ent, means[0], means[1])


def solution(mesh):
    in_specs = (P("req", "vocab"), P(), P(None, ("req", "vocab")), P("req"), P("req", None))
    out_specs = (P(("req", "vocab")), P(("req", "vocab")), P("req"), P("req"))
    return jax.shard_map(shards, mesh=mesh, in_specs=in_specs, out_specs=out_specs, check_vma=False)
```

```python
import functools
import jax
import jax.numpy as jnp
from jax import lax
from jax.experimental import pallas as pl
from jax.experimental.pallas import tpu as pltpu
from jax.sharding import PartitionSpec as P


def stats_kernel(tiles, n_pieces, n_heads, *refs):
    kofs, colbase, side_ref = refs[:3]
    pieces = refs[3 : 3 + n_pieces]
    heads = refs[3 + n_pieces : 3 + n_pieces + n_heads]
    out_ref, x_scr, h_scr, f_scr, t_scr, m_scr, s_scr, w_scr, p_scr, x_sem, h_sem = refs[
        3 + n_pieces + n_heads :
    ]
    step = pl.program_id(0)
    n_tiles, width = len(tiles), h_scr.shape[3]
    firsts = [0]
    for _, columns in tiles:
        firsts.append(firsts[-1] + sum(g[2] for g in columns))
    blocks = [(g[0][0], k) for _, columns in tiles for g in columns for k in range(g[2])]
    same = [k for k in range(1, len(blocks)) if blocks[k] == blocks[k - 1]]

    def is_one_of(at, steps):
        return functools.reduce(jnp.logical_or, [at == k for k in steps], at < 0)

    def slot_of(at):
        return lax.rem(at - sum(((at >= k).astype(jnp.int32) for k in same), jnp.int32(0)), 2)

    slot = slot_of(step)

    def depth_at(j, size):
        return pl.multiple_of(kofs[j], 128) if j >= 0 else (-1 - j) * size

    def row_copies(k):
        return [
            pltpu.make_async_copy(
                pieces[a].at[pl.ds(src, rows)],
                x_scr.at[k % 2, pl.ds(dst, rows), pl.ds(depth_at(j, pieces[a].shape[1]), pieces[a].shape[1])],
                x_sem.at[k % 2],
            )
            for a, j, src, rows, dst in tiles[k][0]
        ]

    def head_copies(parts, block, slot):
        return [
            pltpu.make_async_copy(
                heads[k].at[:, pl.ds(pl.multiple_of(block * width, width), width)],
                h_scr.at[slot, which, pl.ds(n * heads[k].shape[0], heads[k].shape[0])],
                h_sem.at[slot],
            )
            for which in range(2)
            for n, k in enumerate(parts[which])
        ]

    def start_head(at, slot):
        first = 0
        for _, columns in tiles:
            for one, two, blocks in columns:
                @pl.when((at >= first) & (at < first + blocks))
                def _(parts=(one, two), first=first):
                    for copy in head_copies(parts, at - first, slot):
                        copy.start()
                first += blocks

    @pl.when(step == 0)
    def _():
        for copy in row_copies(0):
            copy.start()
        start_head(0, 0)

    for k in range(n_tiles):
        @pl.when(step == firsts[k])
        def _(k=k):
            if k + 1 < n_tiles:
                for copy in row_copies(k + 1):
                    copy.start()
            rows = x_scr.shape[1]
            f_scr[...] = jnp.broadcast_to(side_ref[0:1, :], (128, rows)).T
            lane = lax.broadcasted_iota(jnp.int32, (rows, 128), 1)
            t_scr[...] = jnp.broadcast_to(side_ref[1:2, :], (128, rows)).T.astype(jnp.int32) - lane
            m_scr[...] = jnp.full(m_scr.shape, -jnp.inf, jnp.float32)
            s_scr[...] = jnp.zeros(s_scr.shape, jnp.float32)
            w_scr[...] = jnp.zeros(w_scr.shape, jnp.float32)
            p_scr[...] = jnp.zeros(p_scr.shape, jnp.float32)
            for copy in row_copies(k):
                copy.wait()

    @pl.when((step + 1 < firsts[-1]) & jnp.logical_not(is_one_of(step + 1, same)))
    def _():
        start_head(step + 1, slot_of(step + 1))

    @pl.when(jnp.logical_not(is_one_of(step, same)))
    def _():
        for copy in head_copies(tiles[0][1][0], 0, slot):
            copy.wait()

    held = sum(((step >= f).astype(jnp.int32) for f in firsts[1:-1]), jnp.int32(0))
    rows, sub = x_scr.shape[1], 64

    raws = [
        jnp.dot(x_scr[lax.rem(held, 2)], h_scr[slot, which], preferred_element_type=jnp.float32)
        for which in range(2)
    ]
    bases = [colbase[step * 2 + which] + c for which in range(2) for c in range(0, width, 128)]
    for at in range(0, rows, sub):
        here = pl.ds(at, sub)
        scale, wanted = f_scr[here, :], t_scr[here, :]
        parts = [raw[at : at + sub, c : c + 128] * scale for raw in raws for c in range(0, width, 128)]
        old = m_scr[here, :]
        new = functools.reduce(jnp.maximum, parts, old)
        fade = jnp.exp(old - new)
        total, moment, picked = s_scr[here, :] * fade, w_scr[here, :] * fade, p_scr[here, :]
        for base, part in zip(bases, parts):
            weight = jnp.exp(part - new)
            total += weight
            moment += weight * part
            picked = jnp.where(wanted == base, part, picked)
        m_scr[here, :], s_scr[here, :], w_scr[here, :], p_scr[here, :] = new, total, moment, picked

    for last in firsts[1:]:
        @pl.when(step == last - 1)
        def _():
            peak_t = m_scr[...].T
            peak = jnp.max(peak_t, axis=0, keepdims=True)
            fade = jnp.exp(peak_t - peak)
            out_ref[0:1, :] = peak
            out_ref[1:2, :] = jnp.sum(s_scr[...].T * fade, axis=0, keepdims=True)
            out_ref[2:3, :] = jnp.sum(w_scr[...].T * fade, axis=0, keepdims=True)
            out_ref[3:4, :] = jnp.sum(p_scr[...].T, axis=0, keepdims=True)


def stats(tiles, rows, width, kofs, colbase, side, pieces, heads):
    n_tiles = len(tiles)
    counts = [sum(g[2] for g in columns) for _, columns in tiles]
    firsts = [sum(counts[:k]) for k in range(1, n_tiles)]
    n_steps, depth = sum(counts), heads[0].shape[0]

    def block(step):
        return 0, sum(((step >= f).astype(jnp.int32) for f in firsts), jnp.int32(0))

    return pl.pallas_call(
        functools.partial(stats_kernel, tiles, len(pieces), len(heads)),
        grid=(n_steps,),
        in_specs=[pl.BlockSpec(memory_space=pltpu.SMEM)] * 2
        + [pl.BlockSpec((2, rows), block)]
        + [pl.BlockSpec(memory_space=pl.ANY)] * (len(pieces) + len(heads)),
        out_specs=pl.BlockSpec((4, rows), block),
        out_shape=jax.ShapeDtypeStruct((4, n_tiles * rows), jnp.float32),
        scratch_shapes=[
            pltpu.VMEM((min(n_tiles, 2), rows, depth), jnp.bfloat16),
            pltpu.VMEM((2, 2, depth, width), jnp.bfloat16),
        ]
        + [pltpu.VMEM((rows, 128), jnp.float32), pltpu.VMEM((rows, 128), jnp.int32)]
        + [pltpu.VMEM((rows, 128), jnp.float32)] * 4
        + [pltpu.SemaphoreType.DMA((min(n_tiles, 2),)), pltpu.SemaphoreType.DMA((2,))],
        compiler_params=pltpu.CompilerParams(
            dimension_semantics=("arbitrary",), vmem_limit_bytes=48 * 1024 * 1024
        ),
        cost_estimate=pl.CostEstimate(flops=1 << 20, bytes_accessed=1 << 10, transcendentals=0),
    )(kofs, colbase, side, *pieces, *heads)


EPS = 1e-05
SHRINK = 2.0**-9


def merge(stats):
    peak, total, moment, picked = (stats[:, k] for k in range(4))
    best = jnp.max(peak, axis=0)
    fade = jnp.exp(peak - best[None])
    return jnp.stack(
        [best, jnp.sum(total * fade, axis=0), jnp.sum(moment * fade, axis=0), jnp.sum(picked, axis=0)]
    )


def shards(hidden, gain, head, targets, lengths):
    n_req, n_vocab = lax.axis_size("req"), lax.axis_size("vocab")
    q, v = lax.axis_index("req"), lax.axis_index("vocab")
    spots = n_vocab // 2
    s, c = v // 2, v % 2
    rows, feats = hidden.shape
    depth, cols = head.shape
    blk, half = rows // n_vocab, rows // 2
    cut = half - blk
    every = ("req", "vocab")

    def move(x, where):
        pairs = [
            (a * n_vocab + b, where(a, b)) for a in range(n_req) for b in range(n_vocab)
        ]
        return lax.ppermute(x, every, pairs)

    def to_core(x):
        return move(x, lambda a, b: a * n_vocab + (b ^ 1))

    def to_x(x):
        return move(x, lambda a, b: (a ^ 1) * n_vocab + b)

    def to_y(x):
        return move(x, lambda a, b: (a ^ 2) * n_vocab + b)

    def to_z(x, by):
        return move(x, lambda a, b: a * n_vocab + (b + 2 * by) % n_vocab)

    n_far = 4 if cols % 512 == 0 else 1
    far_cols = cols // n_far
    width = min(256, far_cols)

    def mine(x, core):
        x = lax.dynamic_index_in_dim(x, core, 1, keepdims=False)
        return x.reshape(half, *x.shape[2:])

    token = [None]

    def after(x):
        return x if token[0] is None else lax.optimization_barrier((x, token[0]))[0]

    def step_ends(*results):
        one = results[0][:1, :1].astype(jnp.float32) if token[0] is None else token[0]
        token[0] = lax.optimization_barrier((one, *results))[0]

    blocks = [head[:, :far_cols]]

    def far_part(k):
        return after(blocks[k])

    far = [to_x(far_part(0))]
    raw = hidden.reshape(spots, 2, blk, feats)
    other = to_core(mine(raw, 1 - c))
    one = mine(raw, c)
    values = jnp.where(
        c == 0, jnp.concatenate([one, other], axis=1), jnp.concatenate([other, one], axis=1)
    ).astype(jnp.float32)
    pair_gain = lax.dynamic_slice_in_dim(gain, 2 * s * feats, 2 * feats) * SHRINK
    piece = (values * pair_gain[None, :]).astype(jnp.bfloat16)
    square_sum = jnp.sum(values * values, axis=1).reshape(1, half)
    n_a = half // 2
    a, b = {0: (piece, 0)}, {0: (piece, n_a)}
    ya, yb, far_near = {}, {}, []
    step_ends(other)
    near = to_core(after(head))

    seq_lens = lengths[0, :-1]
    stops = jnp.cumsum(seq_lens)
    starts = stops - seq_lens
    live_rows = jnp.sum(seq_lens)

    trip = [0] + [j for k in range(1, spots // 2 + 1) for j in dict.fromkeys((k, spots - k))]
    z_list = [(ring, j) for ring in (a, b) for j in trip[1:]]
    y_list = [(a, ya, 0), (b, yb, 0)] + [(ring, out, j) for ring, out in ((a, ya), (b, yb)) for j in trip[1:]]
    stage = max(1, len(y_list) // 4)
    doubled = 0
    side = y_side = None
    kofs = (s + spots - jnp.arange(spots, dtype=jnp.int32)) % spots * (2 * feats)

    def group(g):
        if g == 0:
            return head, near, (q * n_vocab + v) * cols, (q * n_vocab + (v ^ 1)) * cols
        at = (g - 1) * far_cols
        return (
            far[g - 1],
            far_near[g - 1],
            ((q ^ 1) * n_vocab + v) * cols + at,
            ((q ^ 1) * n_vocab + (v ^ 1)) * cols + at,
        )

    def call(*wanted):
        tiles, arrays, heads, sides, bases, places = [], [], [], [], [], {}
        for name, chosen in wanted:
            ring = {"A": a, "B": b, "E": ya, "F": yb}[name]
            at = n_a if name in "BF" else 0
            sides.append((side if name in "AB" else y_side)[:, at : at + n_a])
            rows = []
            for j in trip:
                key = next((k for k, x in enumerate(arrays) if x is ring[j][0]), len(arrays))
                places[name, j] = key
                if key == len(arrays):
                    arrays.append(ring[j][0])
                rows.append((places[name, j], j, ring[j][1], n_a, 0))
            columns = []
            for g in chosen:
                one, two, base, pair = group(g)
                for key, array in ((("h", g, 0), one), (("h", g, 1), two)):
                    places.setdefault(key, len(heads))
                    if places[key] == len(heads):
                        heads.append(array)
                blocks = one.shape[1] // width
                columns.append(([places["h", g, 0]], [places["h", g, 1]], blocks))
                for k in range(blocks):
                    bases += [base + k * width, pair + k * width]
            tiles.append((rows, columns))
        out = stats(
            tiles,
            n_a,
            width,
            kofs,
            jnp.stack(bases).astype(jnp.int32),
            after(jnp.concatenate(sides, axis=1)),
            arrays,
            heads,
        )
        for k, (name, _) in enumerate(wanted):
            outs[name].append(out[:, k * n_a : (k + 1) * n_a])
        return out

    outs = {name: [] for name in "ABEF"}
    n_steps = 4
    tiny = square_sum
    for step in range(n_steps):
        ends = []
        if 1 <= step and step + 1 < n_far:
            far.append(to_x(far_part(step + 1)))
        if step and step <= n_far:
            far_near.append(to_core(after(far[step - 1])))
        for n in range(len(z_list) if step == n_steps - 2 else min(stage, len(z_list))):
            ring, j = z_list.pop(0)
            by = 1 if j <= spots // 2 else -1
            array, at = ring[(j - by) % spots]
            array = after(array[at : at + n_a])
            ring[j] = (to_z(array, by), 0)
            ends.append(ring[j][0])
            if step == 0 and n == 0 and n_far > 1:
                rest = lax.optimization_barrier((head, ends[0]))[0]
                blocks += [rest[:, k * far_cols : (k + 1) * far_cols] for k in range(1, n_far)]
                far.append(to_x(blocks[1]))
                ends += blocks[1:]
        if step == n_steps - 1:
            for _, out, j in [y for y in y_list if y[2] > spots // 2]:
                array, at = out[(j + 1) % spots]
                block = first_yb if (j + 1) % spots == 0 else array[at : at + n_a]
                out[j] = (to_z(after(block), -1), 0)
                ends.append(out[j][0])
            y_list = [y for y in y_list if y[2] <= spots // 2]
        batch = [y_list.pop(0) for _ in range(len(y_list) if step == n_steps - 1 else min(stage, len(y_list)))]
        cuts = [[y for y in batch if y[0] is a], [y for y in batch if y[0] is b]] if step == 2 else [batch]
        for part in cuts:
            arrays = [ring[j][0][ring[j][1] : ring[j][1] + n_a] for ring, _, j in part]
            sent = to_y(after(piece if step == 0 and len(part) == 2 else jnp.concatenate(arrays)))
            for n, (_, out, j) in enumerate(part):
                out[j] = (sent, n * n_a)
            ends.append(sent)
        for _ in range(1 if spots == 4 else 5):
            if 2**doubled < spots:
                sent = to_z(lax.optimization_barrier((after(tiny), ends[0]))[0] if step == 0 else after(tiny), 2**doubled)
                tiny = tiny + sent
                doubled += 1
                ends.append(sent)
        if step == 2:
            scale = lax.rsqrt(tiny / depth + EPS) * (1.0 / SHRINK)
            wanted = mine(targets.astype(jnp.float32).reshape(spots, 2, blk), c).reshape(1, half)
            side = jnp.concatenate([scale, wanted])
            y_side = to_y(after(side))
            ends.append(y_side)
        if step == 2:
            many = n_far > 1
            first = call(("A", [0, 1, 2] if many else [0]))
            y_side = lax.optimization_barrier((y_side, first))[0]
            ends.append(call(("E", [0, 1, 2] if many else [0])))
        if step == 3:
            ends.append(call(("B", [0, 1, 2, 3] if many else [0])))
        if step == 0:
            ends += [stops, starts, live_rows]
        if step == n_steps - 2:
            first_yb = after(yb[0][0][yb[0][1] : yb[0][1] + n_a])
            ends.append(first_yb)
        if step < n_steps - 1:
            ends.append(far[min(step, n_far - 1)])
        if step == 0:
            ends.append(near)
        step_ends(*ends)
    if many:
        ends = call(("F", [0, 1, 2, 3]))
        far_near.append(to_core(lax.optimization_barrier((far[3], ends))[0]))
        y_side = lax.optimization_barrier((y_side, ends))[0]
        ends = call(("E", [3]), ("A", [3]))
        y_side = lax.optimization_barrier((y_side, ends))[0]
        call(("F", [4]), ("A", [4]), ("B", [4]), ("E", [4]))
    else:
        call(("F", [0, 1]), ("A", [1]), ("B", [1]), ("E", [1]))
    own = jnp.concatenate([merge(jnp.stack(outs["A"])), merge(jnp.stack(outs["B"]))], axis=1)
    peer = jnp.concatenate([merge(jnp.stack(outs["E"])), merge(jnp.stack(outs["F"]))], axis=1)

    first = q // 2 == 0
    whole = jnp.stack([jnp.where(first, own, peer), jnp.where(first, peer, own)])
    whole = jnp.broadcast_to(whole.reshape(2, 1, 4 * half), (2, spots, 4 * half))
    kin = [
        [(2 * a + b) * n_vocab + 2 * k + core for a in range(2) for k in range(spots)]
        for b in range(2)
        for core in range(2)
    ]
    whole = lax.all_to_all(
        whole.reshape(2 * spots, 4 * half), every, split_axis=0, concat_axis=0, axis_index_groups=kin, tiled=True
    )
    peak, total, moment, picked = merge(whole.reshape(2 * spots, 4, half))
    log_total = peak + jnp.log(total)
    lp, ent = picked - log_total, log_total - moment / total

    local = jnp.arange(half, dtype=jnp.int32)
    local = (local // blk * 2 + c) * blk + local % blk
    member = (local[None, :] >= starts[:, None]) & (local[None, :] < stops[:, None])
    both = jnp.stack([lp, ent])
    sums = jnp.sum(jnp.where(member[None], both[:, None, :], 0.0), axis=2)
    both = lax.optimization_barrier((both, sums))[0]
    valid = v * blk + jnp.arange(blk, dtype=jnp.int32) < live_rows
    lp, ent = jnp.where(valid[None], lax.dynamic_slice_in_dim(both, s * blk, blk, axis=1), 0.0)
    sums = sums + to_core(sums)
    means = sums / seq_lens.astype(jnp.float32)[None]
    return (lp, ent, means[0], means[1])


def solution(mesh):
    in_specs = (P("req", "vocab"), P(), P(None, ("req", "vocab")), P("req"), P("req", None))
    out_specs = (P(("req", "vocab")), P(("req", "vocab")), P("req"), P("req"))
    return jax.shard_map(shards, mesh=mesh, in_specs=in_specs, out_specs=out_specs, check_vma=False)
```
